512 devices in a mesh: frames: 64 (over z, x, core), pix: 8 (over y).
Axes of the slice: x: 4, y: 8, z: 8, core: 2. Of those that a mesh axis runs over, the one named last changes fastest.
Arguments:
- counts: int32 [4096, 65536], P('frames', 'pix'), may hold values from 0 to 64
- weights: float32 [16, 4096], P(None, 'frames'), may hold values from 0.025 to 3, as said below
- maps: float32 [16, 65536], P(None, 'pix'), may hold values from 0.1 to 1
Outputs:
- new_weights: float32 [16, 4096], P(None, 'frames')
- new_maps: float32 [16, 65536], P(None, 'pix')
The draws below stay inside these ranges and needn't reach their ends.
Inputs may be any that keep to these rules, and one draw needn't show every extreme that they name: `weights`: positive.
All inputs are finite; a program needn't handle non-finite values.
Results may differ from the reference program's by a relative error of at most 0.0001.
Values sent between devices are 32-bit elements; how exact they have to be, the bound alone decides.
A program may use at most 64 MiB of HBM per device.

```python
import math
import jax
import jax.numpy as jnp
from jax import lax

K = 16
PIX_DEV = 8192
ITERS = 2
FRAMES = 4096
PIX = 65536
N_PIX = 8


def draw_counts(key, part):
    key = jax.random.fold_in(key, 1)
    first, second, third = jax.random.split(key, 3)
    frame_level = jax.random.randint(first, (FRAMES, 1), 1, 5)
    pixel_level = jax.random.randint(second, (1, PIX), 1, 9)
    rate = frame_level * pixel_level
    values = jax.random.randint(third, (FRAMES, PIX), 0, 2 * rate + 1)
    return values.at[0, 0].set(64).astype(jnp.int32)


def draw_weights(key, part):
    key = jax.random.fold_in(key, 2)
    place = jnp.arange(FRAMES, dtype=jnp.float32)[None, :] / (FRAMES - 1)
    base = jax.random.uniform(key, (K, FRAMES), jnp.float32, 0.05, 0.2)
    level = 10.0 ** place
    return (base * level).astype(jnp.float32)


def levels(rng, dims, cuts, smallest, largest):
    loudness = 1.0
    for axis_at, blocks in cuts:
        steps = jax.random.uniform(jax.random.fold_in(jax.random.fold_in(rng, 6), axis_at), (blocks,), jnp.float32, smallest / len(cuts), largest / len(cuts))
        loudness = loudness * jnp.repeat(jnp.exp(steps), dims[axis_at] // blocks).reshape((-1,) + (1,) * (len(dims) - 1 - axis_at))
    return loudness


def setup_inputs(seed: int = 0) -> dict:
    keys = jax.random.split(jax.random.key(seed), 4)
    counts = draw_counts(jax.random.fold_in(keys[3], 71), 0)
    weights = draw_weights(jax.random.fold_in(keys[3], 71), 0)
    maps = jnp.clip(jnp.exp(math.log(1.0) - 2.3025851 * jax.random.uniform(keys[2], (K, PIX), jnp.float32) ** levels(keys[2], (K, PIX), ((1, 8),), -0.2, 0.2)), 0.1, 1.0)
    return {"counts": counts, "weights": weights, "maps": maps}


def reference(counts, weights, maps):
    high = lax.Precision.HIGHEST
    wmat = weights
    hmat = maps
    for step in range(ITERS):
        wsum = jnp.sum(wmat, axis=1)

        def update_block(index, hcur):
            start = (index * PIX_DEV).astype(jnp.int32)
            block = lax.dynamic_slice_in_dim(counts, start, PIX_DEV, 1).astype(jnp.float32)
            hblock = lax.dynamic_slice_in_dim(hcur, start, PIX_DEV, 1)
            model = jnp.dot(wmat.T, hblock, precision=high)
            numer = jnp.dot(wmat, block / model, precision=high)
            return lax.dynamic_update_slice_in_dim(hcur, hblock * numer / wsum[:, None], start, 1)

        hmat = lax.fori_loop(0, N_PIX, update_block, hmat)
        hsum = jnp.sum(hmat, axis=1)

        def add_block(index, total):
            start = (index * PIX_DEV).astype(jnp.int32)
            block = lax.dynamic_slice_in_dim(counts, start, PIX_DEV, 1).astype(jnp.float32)
            hblock = lax.dynamic_slice_in_dim(hmat, start, PIX_DEV, 1)
            model = jnp.dot(wmat.T, hblock, precision=high)
            return total + lax.dot_general(hblock, block / model, (((1,), (1,)), ((), ())), precision=high)

        wnum = lax.fori_loop(0, N_PIX, add_block, jnp.zeros(wmat.shape, jnp.float32))
        wmat = wmat * wnum / hsum[:, None]
    return wmat, hmat
```

```python
import functools

import jax
import jax.numpy as jnp
from jax import lax
from jax.experimental import pallas as pl
from jax.experimental.pallas import tpu as pltpu
from jax.sharding import PartitionSpec as P

MESH = pl.DeviceIdType.MESH
F32 = jnp.float32
BF16 = jnp.bfloat16
ITERS = 2
NZ, NX, NY = 8, 4, 8
K = 16
LANES = 128
FRAMES = 64
HALF = NZ * NX
PIECE = 16
PIX = 2 * HALF * LANES


def hops(offset):
    dz, dx = offset
    return min(dz, NZ - dz) + min(dx, NX - dx)


OFFSETS = sorted(((dz, dx) for dz in range(NZ) for dx in range(NX) if dz or dx), key=lambda o: -hops(o))
SLOT = {offset: i for i, offset in enumerate(OFFSETS)}
Y_OFFSETS = (4, 3, 5, 2, 6, 1, 7)


def split(x):
    hi = x.astype(BF16)
    return hi, (x - hi.astype(F32)).astype(BF16)


def weight_operands(w):
    hi, lo = split(w)
    for_model = jnp.concatenate([hi, hi, lo, lo], axis=0)
    for_maps = jnp.concatenate([jnp.concatenate([hi, hi], axis=1), jnp.concatenate([lo, lo], axis=1)], axis=0)
    return for_model, for_maps


def load_maps(h_ref, first, count):
    return jnp.concatenate([h_ref[first + i] for i in range(count)], axis=1)


def ratios(c_ref, h, for_model, first, count):
    hi, lo = split(h)
    model = lax.dot_general(
        for_model,
        jnp.concatenate([hi, lo, hi, lo], axis=0),
        (((0,), (0,)), ((), ())),
        preferred_element_type=F32,
    )
    width = count * LANES
    counts = c_ref[:, pl.ds(pl.multiple_of(first * LANES, width), width)].astype(F32)
    r_hi, r_lo = split(counts / model)
    return jnp.concatenate([r_hi, r_lo], axis=0), jnp.concatenate([hi, lo], axis=0)


def to_row(column):
    shape = (K, LANES)
    diagonal = lax.broadcasted_iota(jnp.int32, shape, 0) == lax.broadcasted_iota(jnp.int32, shape, 1)
    return jnp.sum(jnp.where(diagonal, column, 0.0), axis=0, keepdims=True)


def to_column(row):
    shape = (K, LANES)
    diagonal = lax.broadcasted_iota(jnp.int32, shape, 0) == lax.broadcasted_iota(jnp.int32, shape, 1)
    return jnp.sum(jnp.where(diagonal, row, 0.0), axis=1, keepdims=True)


def kernel(
    c_hbm, w_ref, h_hbm, w_out, h_out,
    c_ref, h_in, h_ref, numer, from_core, partial, parts, chunk_sum, row_src, row_core, row_sum, rows, y_src, y_parts,
    load_sem, core_send, core_recv, part_send, part_recv, map_send, map_recv, half_send, half_recv,
    rowc_send, rowc_recv, row_send, row_recv, y_send, y_recv,
):
    f = lax.axis_index("frames")
    y = lax.axis_index("pix")
    z, x, core = f // (2 * NX), lax.rem(f // 2, NX), lax.rem(f, 2)

    def device(dz, dx):
        zz, xx = lax.rem(z + dz, NZ), lax.rem(x + dx, NX)
        return zz * NX + xx, ((zz * NX + xx) * 2 + core, y)

    sibling = (f + 1 - 2 * core, y)
    y_devices = [(f, lax.rem(y + d, NY)) for d in Y_OFFSETS]

    own_half = pl.multiple_of(core * HALF, HALF)
    other_half = pl.multiple_of((1 - core) * HALF, HALF)
    own = z * NX + x

    barrier = pltpu.get_barrier_semaphore()
    for offset in OFFSETS:
        pl.semaphore_signal(barrier, inc=1, device_id=device(*offset)[1], device_id_type=MESH)
    for d in [sibling] + y_devices:
        pl.semaphore_signal(barrier, inc=1, device_id=d, device_id_type=MESH)

    loads = []
    for i, first in enumerate((other_half, own_half)):
        columns = pl.ds(pl.multiple_of(first * LANES, HALF * LANES), HALF * LANES)
        loads.append(pltpu.make_async_copy(h_hbm.at[:, columns], h_in.at[:, columns], load_sem.at[2 * i]))
        loads.append(pltpu.make_async_copy(c_hbm.at[:, columns], c_ref.at[:, columns], load_sem.at[2 * i + 1]))
    for load in loads:
        load.start()

    def unpack(first):
        for i in range(HALF):
            column = pl.multiple_of((first + i) * LANES, LANES)
            h_ref[0, first + i] = h_in[:, pl.ds(column, LANES)]

    def remote(src, dst, send, recv, to):
        return pltpu.make_async_remote_copy(
            src_ref=src, dst_ref=dst, send_sem=send, recv_sem=recv, device_id=to, device_id_type=MESH
        )

    w = w_ref[...]
    for it in range(ITERS):
        h_now, h_next = h_ref.at[it], h_ref.at[it + 1]
        for_model, for_maps = weight_operands(w)
        w_total = jnp.sum(w, axis=1, keepdims=True)
        row_src[it] = to_row(w_total)

        def numerators(first, at, out):
            rc, _ = ratios(c_ref, load_maps(h_now, first + at, PIECE), for_model, first + at, PIECE)
            both = jnp.dot(for_maps, rc, preferred_element_type=F32)
            both = both[:K] + both[K:]
            for i in range(PIECE):
                out[at + i] = both[:, i * LANES : (i + 1) * LANES]

        if it == 0:
            loads[0].wait()
            loads[1].wait()
            unpack(other_half)
        else:
            row_copy = remote(row_src.at[it], row_core.at[it], rowc_send.at[it], rowc_recv.at[it], sibling)
            row_copy.start()
        core_copies = []
        for piece in range(HALF // PIECE):
            numerators(other_half, piece * PIECE, numer.at[it])
            if it == 0 and piece == 0:
                pl.semaphore_wait(barrier, len(OFFSETS) + 1 + len(y_devices))
                row_copy = remote(row_src.at[it], row_core.at[it], rowc_send.at[it], rowc_recv.at[it], sibling)
                row_copy.start()
            chunks = pl.ds(piece * PIECE, PIECE)
            copy = remote(
                numer.at[it, chunks], from_core.at[it, chunks],
                core_send.at[it, piece], core_recv.at[it, piece], sibling,
            )
            copy.start()
            core_copies.append(copy)
        if it == 0:
            loads[2].wait()
            loads[3].wait()
            unpack(own_half)
        for piece in range(HALF // PIECE):
            numerators(own_half, piece * PIECE, partial.at[it])

        row_copy.wait()
        row_sum[it] = row_src[it] + row_core[it]
        for offset in OFFSETS:
            remote(
                row_sum.at[it], rows.at[it, SLOT[offset]], row_send.at[it], row_recv.at[it], device(*offset)[1]
            ).start()
        for piece, copy in enumerate(core_copies):
            copy.wait()
            chunks = pl.ds(piece * PIECE, PIECE)
            partial[it, chunks] = partial[it, chunks] + from_core[it, chunks]
        for offset in OFFSETS:
            chunk, to = device(*offset)
            remote(
                partial.at[it, chunk], parts.at[it, SLOT[offset]], part_send.at[it], part_recv.at[it], to
            ).start()
        pltpu.make_async_copy(rows.at[it], rows.at[it], row_recv.at[it]).wait()
        pltpu.make_async_copy(rows.at[it], rows.at[it], row_send.at[it]).wait()
        c_total = to_column(row_sum[it] + jnp.sum(rows[it], axis=0))
        pltpu.make_async_copy(parts.at[it], parts.at[it], part_recv.at[it]).wait()
        numer_total = partial[it, own] + jnp.sum(parts[it], axis=0)
        mine = own_half + own
        h_next[mine] = h_now[mine] * numer_total / c_total

        for offset in OFFSETS:
            _, to = device(*offset)
            remote(h_next.at[mine], h_next.at[mine], map_send.at[it], map_recv.at[it], to).start()
        pltpu.make_async_copy(parts.at[it], parts.at[it], part_send.at[it]).wait()
        pltpu.make_async_copy(parts.at[it], parts.at[it], map_recv.at[it]).wait()
        half = h_next.at[pl.ds(own_half, HALF)]
        half_copy = remote(half, half, half_send.at[it], half_recv.at[it], sibling)
        half_copy.start()

        def weight_numerators(first, total, sums):
            for piece in range(HALF // PIECE):
                at = first + piece * PIECE
                h = load_maps(h_next, at, PIECE)
                rc, hc = ratios(c_ref, h, for_model, at, PIECE)
                total += lax.dot_general(hc, rc, (((1,), (1,)), ((), ())), preferred_element_type=F32)
                for i in range(PIECE):
                    sums += h[:, i * LANES : (i + 1) * LANES]
            return total, sums

        total, sums = weight_numerators(own_half, jnp.zeros((2 * K, 2 * FRAMES), F32), jnp.zeros((K, LANES), F32))
        half_copy.wait_recv()
        total, sums = weight_numerators(other_half, total, sums)
        total = total[:K] + total[K:]
        total = total[:, :FRAMES] + total[:, FRAMES:]
        h_total = jnp.sum(sums, axis=1, keepdims=True)
        y_src[it] = jnp.concatenate([total, jnp.broadcast_to(h_total, (K, LANES - FRAMES))], axis=1)
        for i, to in enumerate(y_devices):
            remote(y_src.at[it], y_parts.at[it, i], y_send.at[it], y_recv.at[it], to).start()
        pltpu.make_async_copy(parts.at[it], parts.at[it], map_send.at[it]).wait()
        half_copy.wait_send()
        if it == ITERS - 1:
            for i in range(2 * HALF):
                h_out[:, i * LANES : (i + 1) * LANES] = h_next[i]
        pltpu.make_async_copy(y_parts.at[it], y_parts.at[it], y_recv.at[it]).wait()
        pltpu.make_async_copy(y_parts.at[it], y_parts.at[it], y_send.at[it]).wait()
        total = y_src[it] + jnp.sum(y_parts[it], axis=0)
        w = w * total[:, :FRAMES] / total[:, FRAMES : FRAMES + 1]
    w_out[...] = w


def local(counts, weights, maps):
    n = len(OFFSETS)
    dma = pltpu.SemaphoreType.DMA
    pieces = HALF // PIECE
    return pl.pallas_call(
        kernel,
        out_shape=(jax.ShapeDtypeStruct(weights.shape, F32), jax.ShapeDtypeStruct(maps.shape, F32)),
        in_specs=[
            pl.BlockSpec(memory_space=pl.ANY),
            pl.BlockSpec(memory_space=pltpu.VMEM),
            pl.BlockSpec(memory_space=pl.ANY),
        ],
        out_specs=(pl.BlockSpec(memory_space=pltpu.VMEM), pl.BlockSpec(memory_space=pltpu.VMEM)),
        scratch_shapes=[
            pltpu.VMEM((FRAMES, PIX), jnp.int32),
            pltpu.VMEM((K, PIX), F32),
            pltpu.VMEM((ITERS + 1, 2 * HALF, K, LANES), F32),
            pltpu.VMEM((ITERS, HALF, K, LANES), F32),
            pltpu.VMEM((ITERS, HALF, K, LANES), F32),
            pltpu.VMEM((ITERS, HALF, K, LANES), F32),
            pltpu.VMEM((ITERS, n, K, LANES), F32),
            pltpu.VMEM((K, LANES), F32),
            pltpu.VMEM((ITERS, 1, LANES), F32),
            pltpu.VMEM((ITERS, 1, LANES), F32),
            pltpu.VMEM((ITERS, 1, LANES), F32),
            pltpu.VMEM((ITERS, n, 1, LANES), F32),
            pltpu.VMEM((ITERS, K, LANES), F32),
            pltpu.VMEM((ITERS, NY - 1, K, LANES), F32),
            dma((4,)),
            dma((ITERS, pieces)),
            dma((ITERS, pieces)),
            dma((ITERS,)),
            dma((ITERS,)),
            dma((ITERS,)),
            dma((ITERS,)),
            dma((ITERS,)),
            dma((ITERS,)),
            dma((ITERS,)),
            dma((ITERS,)),
            dma((ITERS,)),
            dma((ITERS,)),
            dma((ITERS,)),
            dma((ITERS,)),
        ],
        compiler_params=pltpu.CompilerParams(
            collective_id=0, has_side_effects=True, vmem_limit_bytes=32 * 1024 * 1024
        ),
        name="nmf_updates",
    )(counts, weights, maps)


def solution(mesh):
    return jax.shard_map(
        local,
        mesh=mesh,
        in_specs=(P("frames", "pix"), P(None, "frames"), P(None, "pix")),
        out_specs=(P(None, "frames"), P(None, "pix")),
        check_vma=False,
    )
```

```python
import functools

import jax
import jax.numpy as jnp
from jax import lax
from jax.experimental import pallas as pl
from jax.experimental.pallas import tpu as pltpu
from jax.sharding import PartitionSpec as P

MESH = pl.DeviceIdType.MESH
F32 = jnp.float32
BF16 = jnp.bfloat16
ITERS = 2
NZ, NX, NY = 8, 4, 8
K = 16
LANES = 128
FRAMES = 64
HALF = NZ * NX
PIX = 2 * HALF * LANES


def hops(offset):
    dz, dx = offset
    return min(dz, NZ - dz) + min(dx, NX - dx)


OFFSETS = sorted(((dz, dx) for dz in range(NZ) for dx in range(NX) if dz or dx), key=lambda o: (-min(o[1], NX - o[1]), -min(o[0], NZ - o[0])))
SLOT = {offset: i for i, offset in enumerate(OFFSETS)}
Y_OFFSETS = (4, 3, 5, 2, 6, 1, 7)
FAR_FIRST = (4, 3, 5, 2, 6, 1, 7, 0)
NEAR_FIRST = (0, 1, 7, 2, 6, 3, 5, 4)
GROUPS = 4
PIECES = NZ // GROUPS
GROUP_PIX = NX * LANES
PIECE = GROUPS * NX
PARTS = 2
ROWS = K // PARTS


def split(x):
    hi = x.astype(BF16)
    return hi, (x - hi.astype(F32)).astype(BF16)


def weight_operands(w):
    hi, lo = split(w)
    for_model = jnp.concatenate([hi, hi, lo, lo], axis=0)
    for_maps = jnp.concatenate([jnp.concatenate([hi, hi], axis=1), jnp.concatenate([lo, lo], axis=1)], axis=0)
    return for_model, for_maps


def columns(chunk, count):
    return pl.ds(pl.multiple_of(chunk * LANES, count * LANES), count * LANES)


def ratios(c_ref, h, for_model, firsts):
    hi, lo = split(h)
    model = lax.dot_general(
        for_model,
        jnp.concatenate([hi, lo, hi, lo], axis=0),
        (((0,), (0,)), ((), ())),
        preferred_element_type=F32,
    )
    counts = jnp.concatenate([c_ref[:, columns(q, NX)] for q in firsts], axis=1).astype(F32)
    r_hi, r_lo = split(counts / model)
    return jnp.concatenate([r_hi, r_lo], axis=0), jnp.concatenate([hi, lo], axis=0)


def to_row(column):
    shape = (K, LANES)
    diagonal = lax.broadcasted_iota(jnp.int32, shape, 0) == lax.broadcasted_iota(jnp.int32, shape, 1)
    return jnp.sum(jnp.where(diagonal, column, 0.0), axis=0, keepdims=True)


def to_column(row):
    shape = (K, LANES)
    diagonal = lax.broadcasted_iota(jnp.int32, shape, 0) == lax.broadcasted_iota(jnp.int32, shape, 1)
    return jnp.sum(jnp.where(diagonal, row, 0.0), axis=1, keepdims=True)


def kernel(
    c_hbm, w_hbm, h_hbm, w_out, h_out,
    c_ref, w_ref, h_in, h_ref, numer, from_core, partial, parts, row_src, row_core, row_sum, rows, y_src, y_parts,
    load_sem, core_send, core_recv, part_send, part_recv, map_send, map_recv, half_send, half_recv,
    rowc_send, rowc_recv, row_send, row_recv, y_send, y_recv,
):
    f = lax.axis_index("frames")
    y = lax.axis_index("pix")
    z, x, core = f // (2 * NX), lax.rem(f // 2, NX), lax.rem(f, 2)
    around_z = [lax.rem(z + d, NZ) for d in range(NZ)]
    around_x = [lax.rem(x + d, NX) for d in range(NX)]

    def device(dz, dx):
        return ((around_z[dz] * NX + around_x[dx]) * 2 + core, y)

    sibling = (f + 1 - 2 * core, y)
    y_devices = [(f, lax.rem(y + d, NY)) for d in Y_OFFSETS]
    own_half = core * HALF
    other_half = (1 - core) * HALF
    mine = own_half + z * NX + x

    barrier = pltpu.get_barrier_semaphore()
    for offset in OFFSETS:
        pl.semaphore_signal(barrier, inc=1, device_id=device(*offset), device_id_type=MESH)
    for d in [sibling] + y_devices:
        pl.semaphore_signal(barrier, inc=1, device_id=d, device_id_type=MESH)

    def piece_firsts(half, order, piece):
        return [half + around_z[dz] * NX for dz in order[piece * GROUPS : (piece + 1) * GROUPS]]

    load_w = pltpu.make_async_copy(w_hbm, w_ref, load_sem.at[0])
    load_h = pltpu.make_async_copy(h_hbm, h_in, load_sem.at[1])
    load_w.start()
    load_h.start()
    loads = {}
    n = 2
    for half in (1, 0):
        for piece in range(PIECES):
            loads[half, piece] = []
            for q in piece_firsts((own_half, other_half)[half], FAR_FIRST, piece):
                copy = pltpu.make_async_copy(c_hbm.at[:, columns(q, NX)], c_ref.at[:, columns(q, NX)], load_sem.at[n])
                copy.start()
                loads[half, piece].append(copy)
                n += 1

    def remote(src, dst, send, recv, to):
        return pltpu.make_async_remote_copy(
            src_ref=src, dst_ref=dst, send_sem=send, recv_sem=recv, device_id=to, device_id_type=MESH
        )

    load_w.wait()
    load_h.wait()
    w = w_ref[...]
    for it in range(ITERS):
        h_next = h_ref.at[it]

        def maps_at(q, count):
            if it == 0:
                return h_in[:, columns(q, count)]
            return jnp.concatenate([h_ref[it - 1, q + i] for i in range(count)], axis=1)

        for_model, for_maps = weight_operands(w)
        row_src[it] = to_row(jnp.sum(w, axis=1, keepdims=True))

        def numerators(half, piece, out):
            firsts = piece_firsts((own_half, other_half)[half], FAR_FIRST, piece)
            if it == 0:
                for copy in loads[half, piece]:
                    copy.wait()
            h = jnp.concatenate([maps_at(q, NX) for q in firsts], axis=1)
            rc, _ = ratios(c_ref, h, for_model, firsts)
            both = jnp.dot(for_maps, rc, preferred_element_type=F32)
            both = both[:K] + both[K:]
            for i in range(PIECE):
                out[piece * PIECE + i] = both[:, i * LANES : (i + 1) * LANES]

        def send_parts(here, part):
            band = pl.ds(part * ROWS, ROWS)
            for dz, dx in OFFSETS:
                if dz in here:
                    remote(
                        partial.at[it, FAR_FIRST.index(dz) * NX + around_x[dx], band],
                        parts.at[it, part, SLOT[dz, dx]],
                        part_send.at[it], part_recv.at[it, part], device(dz, dx),
                    ).start()

        row_copy = remote(row_src.at[it], row_core.at[it], rowc_send.at[it], rowc_recv.at[it], sibling)
        if it:
            row_copy.start()
        core_copies = []
        for piece in range(PIECES):
            numerators(1, piece, numer.at[it])
            if it == 0 and piece == 0:
                pl.semaphore_wait(barrier, len(OFFSETS) + 1 + len(y_devices))
                row_copy.start()
            chunks = pl.ds(piece * PIECE, PIECE)
            copy = remote(
                numer.at[it, chunks], from_core.at[it, chunks],
                core_send.at[it, piece], core_recv.at[it, piece], sibling,
            )
            copy.start()
            core_copies.append(copy)
        for piece in range(PIECES):
            numerators(0, piece, partial.at[it])
            if piece == 0:
                row_copy.wait()
                row_sum[it] = row_src[it] + row_core[it]
                for offset in OFFSETS:
                    remote(
                        row_sum.at[it], rows.at[it, SLOT[offset]], row_send.at[it], row_recv.at[it], device(*offset)
                    ).start()
            core_copies[piece].wait()
            chunks = pl.ds(piece * PIECE, PIECE)
            partial[it, chunks] = partial[it, chunks] + from_core[it, chunks]
            send_parts(FAR_FIRST[piece * GROUPS : (piece + 1) * GROUPS], 0)
        for part in range(1, PARTS):
            send_parts(FAR_FIRST, part)

        pltpu.make_async_copy(rows.at[it], rows.at[it], row_recv.at[it]).wait()
        c_total = to_column(row_sum[it] + jnp.sum(rows[it], axis=0))
        scale = maps_at(mine, 1) / c_total
        for part in range(PARTS):
            band = pl.ds(part * ROWS, ROWS)
            landed = parts.at[it, part]
            pltpu.make_async_copy(landed, landed, part_recv.at[it, part]).wait()
            numer_total = partial[it, FAR_FIRST.index(0) * NX + x, band] + jnp.sum(parts[it, part], axis=0)
            h_next[mine, band] = scale[part * ROWS : (part + 1) * ROWS] * numer_total
            chunk = h_next.at[mine, band]
            for dz, dx in OFFSETS:
                remote(chunk, chunk, map_send.at[it], map_recv.at[it, (NZ - dz) % NZ], device(dz, dx)).start()

        total, sums = jnp.zeros((2 * K, 2 * FRAMES), F32), jnp.zeros((K, LANES), F32)

        def weight_numerators(half, piece, total, sums):
            firsts = piece_firsts((own_half, other_half)[half], NEAR_FIRST, piece)
            h = jnp.concatenate([h_next[q + i] for q in firsts for i in range(NX)], axis=1)
            rc, hc = ratios(c_ref, h, for_model, firsts)
            total += lax.dot_general(hc, rc, (((1,), (1,)), ((), ())), preferred_element_type=F32)
            for i in range(PIECE):
                sums += h[:, i * LANES : (i + 1) * LANES]
            return total, sums

        half_copies = []
        for piece in range(PIECES):
            for dz in NEAR_FIRST[piece * GROUPS : (piece + 1) * GROUPS]:
                group = h_next.at[pl.ds(own_half + around_z[dz] * NX, NX)]
                landed = group if dz else parts.at[it, :, pl.ds(0, NX - 1)]
                pltpu.make_async_copy(landed, landed, map_recv.at[it, dz]).wait()
                copy = remote(group, group, half_send.at[it, dz], half_recv.at[it, dz], sibling)
                copy.start()
                half_copies.append(copy)
            total, sums = weight_numerators(0, piece, total, sums)
        for piece in range(PIECES):
            for copy in half_copies[piece * GROUPS : (piece + 1) * GROUPS]:
                copy.wait_recv()
            total, sums = weight_numerators(1, piece, total, sums)
        total = total[:K] + total[K:]
        total = total[:, :FRAMES] + total[:, FRAMES:]
        h_total = jnp.sum(sums, axis=1, keepdims=True)
        y_src[it] = jnp.concatenate([total, jnp.broadcast_to(h_total, (K, LANES - FRAMES))], axis=1)
        for i, to in enumerate(y_devices):
            remote(y_src.at[it], y_parts.at[it, i], y_send.at[it], y_recv.at[it], to).start()
        if it == ITERS - 1:
            for i in range(2 * HALF):
                h_in[:, i * LANES : (i + 1) * LANES] = h_next[i]
            store_h = pltpu.make_async_copy(h_in, h_out, load_sem.at[0])
            store_h.start()
        pltpu.make_async_copy(rows.at[it], rows.at[it], row_send.at[it]).wait()
        pltpu.make_async_copy(parts.at[it], parts.at[it], part_send.at[it]).wait()
        pltpu.make_async_copy(parts.at[it], parts.at[it], map_send.at[it]).wait()
        for copy in half_copies:
            copy.wait_send()
        pltpu.make_async_copy(y_parts.at[it], y_parts.at[it], y_recv.at[it]).wait()
        total = y_src[it] + jnp.sum(y_parts[it], axis=0)
        w = w * total[:, :FRAMES] / total[:, FRAMES : FRAMES + 1]
        pltpu.make_async_copy(y_parts.at[it], y_parts.at[it], y_send.at[it]).wait()
    w_out[...] = w
    store_h.wait()


def local(counts, weights, maps):
    n = len(OFFSETS)
    dma = pltpu.SemaphoreType.DMA
    anywhere = pl.BlockSpec(memory_space=pl.ANY)
    w_new, h_new = pl.pallas_call(
        kernel,
        out_shape=(jax.ShapeDtypeStruct(weights.shape, F32), jax.ShapeDtypeStruct(maps.shape, F32)),
        in_specs=[anywhere] * 3,
        out_specs=(pl.BlockSpec(memory_space=pltpu.VMEM), anywhere),
        scratch_shapes=[
            pltpu.VMEM((FRAMES, PIX), jnp.int32),
            pltpu.VMEM((K, FRAMES), F32),
            pltpu.VMEM((K, PIX), F32),
            pltpu.VMEM((ITERS, 2 * HALF, K, LANES), F32),
            pltpu.VMEM((ITERS, HALF, K, LANES), F32),
            pltpu.VMEM((ITERS, HALF, K, LANES), F32),
            pltpu.VMEM((ITERS, HALF, K, LANES), F32),
            pltpu.VMEM((ITERS, PARTS, n, ROWS, LANES), F32),
            pltpu.VMEM((ITERS, 1, LANES), F32),
            pltpu.VMEM((ITERS, 1, LANES), F32),
            pltpu.VMEM((ITERS, 1, LANES), F32),
            pltpu.VMEM((ITERS, n, 1, LANES), F32),
            pltpu.VMEM((ITERS, K, LANES), F32),
            pltpu.VMEM((ITERS, NY - 1, K, LANES), F32),
            dma((2 + 2 * NZ,)),
            dma((ITERS, PIECES)),
            dma((ITERS, PIECES)),
            dma((ITERS,)),
            dma((ITERS, PARTS)),
            dma((ITERS,)),
            dma((ITERS, NZ)),
            dma((ITERS, NZ)),
            dma((ITERS, NZ)),
            dma((ITERS,)),
            dma((ITERS,)),
            dma((ITERS,)),
            dma((ITERS,)),
            dma((ITERS,)),
            dma((ITERS,)),
        ],
        compiler_params=pltpu.CompilerParams(
            collective_id=0, has_side_effects=True, vmem_limit_bytes=53 * 1024 * 1024
        ),
        name="nmf_updates",
    )(counts, weights, maps)
    return pl.pallas_call(
        store,
        out_shape=(jax.ShapeDtypeStruct(weights.shape, F32), jax.ShapeDtypeStruct(maps.shape, F32)),
        in_specs=[pl.BlockSpec(memory_space=pltpu.VMEM)] * 2,
        out_specs=(anywhere, anywhere),
        scratch_shapes=[dma((2,))],
        compiler_params=pltpu.CompilerParams(vmem_limit_bytes=4 * 1024 * 1024),
        name="store_outputs",
    )(w_new, h_new)


def store(w_in, h_in, w_out, h_out, sems):
    copies = [pltpu.make_async_copy(w_in, w_out, sems.at[0]), pltpu.make_async_copy(h_in, h_out, sems.at[1])]
    for copy in copies:
        copy.start()
    for copy in copies:
        copy.wait()


def solution(mesh):
    return jax.shard_map(
        local,
        mesh=mesh,
        in_specs=(P("frames", "pix"), P(None, "frames"), P(None, "pix")),
        out_specs=(P(None, "frames"), P(None, "pix")),
        check_vma=False,
    )
```

```python
import functools

import jax
import jax.numpy as jnp
from jax import lax
from jax.experimental import pallas as pl
from jax.experimental.pallas import tpu as pltpu
from jax.sharding import PartitionSpec as P

MESH = pl.DeviceIdType.MESH
F32 = jnp.float32
BF16 = jnp.bfloat16
ITERS = 2
NZ, NX, NY = 8, 4, 8
K = 16
LANES = 128
FRAMES = 64
HALF = NZ * NX
PIX = 2 * HALF * LANES


def hops(offset):
    dz, dx = offset
    return min(dz, NZ - dz) + min(dx, NX - dx)


OFFSETS = sorted(((dz, dx) for dz in range(NZ) for dx in range(NX) if dz or dx), key=lambda o: (-min(o[1], NX - o[1]), -min(o[0], NZ - o[0])))
SLOT = {offset: i for i, offset in enumerate(OFFSETS)}
Y_OFFSETS = (4, 3, 5, 2, 6, 1, 7)
FAR_FIRST = (4, 3, 5, 2, 6, 1, 7, 0)
NEAR_FIRST = (0, 1, 7, 2, 6, 3, 5, 4)
GROUPS = 4
PIECES = NZ // GROUPS
GROUP_PIX = NX * LANES
PIECE = GROUPS * NX
PARTS = 2
VIA_X = (4, 3, 5, 2, 6, 1, 7)
VIA_Z = (4, 3, 5, 2, 6, 1, 7)
ROWS = K // PARTS
LAST = PARTS - 1
STAGED = max(1, len(VIA_X))
X_OFFSETS = (2, 1, 3)
PART_OFFSETS = [[o for o in OFFSETS if part < LAST or o[0] not in VIA_X] for part in range(PARTS)]


def split(x):
    hi = x.astype(BF16)
    return hi, (x - hi.astype(F32)).astype(BF16)


def weight_operands(w):
    hi, lo = split(w)
    for_model = jnp.concatenate([hi, hi, lo, lo], axis=0)
    for_maps = jnp.concatenate([jnp.concatenate([hi, hi], axis=1), jnp.concatenate([lo, lo], axis=1)], axis=0)
    return for_model, for_maps


def columns(chunk, count):
    return pl.ds(pl.multiple_of(chunk * LANES, count * LANES), count * LANES)


def ratios(c_ref, h, for_model, firsts):
    hi, lo = split(h)
    model = lax.dot_general(
        for_model,
        jnp.concatenate([hi, lo, hi, lo], axis=0),
        (((0,), (0,)), ((), ())),
        preferred_element_type=F32,
    )
    counts = jnp.concatenate([c_ref[:, columns(q, NX)] for q in firsts], axis=1).astype(F32)
    r_hi, r_lo = split(counts / model)
    return jnp.concatenate([r_hi, r_lo], axis=0), jnp.concatenate([hi, lo], axis=0)


def to_row(column):
    shape = (K, LANES)
    diagonal = lax.broadcasted_iota(jnp.int32, shape, 0) == lax.broadcasted_iota(jnp.int32, shape, 1)
    return jnp.sum(jnp.where(diagonal, column, 0.0), axis=0, keepdims=True)


def to_column(row):
    shape = (K, LANES)
    diagonal = lax.broadcasted_iota(jnp.int32, shape, 0) == lax.broadcasted_iota(jnp.int32, shape, 1)
    return jnp.sum(jnp.where(diagonal, row, 0.0), axis=1, keepdims=True)


def kernel(
    c_hbm, w_hbm, h_hbm, w_out, h_out,
    c_ref, w_ref, h_in, h_ref, numer, from_core, partial, parts, row_src, row_core, row_sum, rows, y_src, y_parts,
    along_x, x_sum, along_z, along_x_send, along_x_recv, along_z_send, along_z_recv, first_send, first_recv,
    load_sem, core_send, core_recv, part_send, part_recv, map_send, map_recv, half_send, half_recv,
    rowc_send, rowc_recv, row_send, row_recv, y_send, y_recv,
):
    f = lax.axis_index("frames")
    y = lax.axis_index("pix")
    z, x, core = f // (2 * NX), lax.rem(f // 2, NX), lax.rem(f, 2)
    around_z = [lax.rem(z + d, NZ) for d in range(NZ)]
    around_x = [lax.rem(x + d, NX) for d in range(NX)]

    def device(dz, dx):
        return ((around_z[dz] * NX + around_x[dx]) * 2 + core, y)

    sibling = (f + 1 - 2 * core, y)
    y_devices = [(f, lax.rem(y + d, NY)) for d in Y_OFFSETS]
    own_half = core * HALF
    last_band = pl.ds(LAST * ROWS, ROWS)
    other_half = (1 - core) * HALF
    mine = own_half + z * NX + x

    barrier = pltpu.get_barrier_semaphore()
    for offset in OFFSETS:
        pl.semaphore_signal(barrier, inc=1, device_id=device(*offset), device_id_type=MESH)
    for d in [sibling] + y_devices:
        pl.semaphore_signal(barrier, inc=1, device_id=d, device_id_type=MESH)

    def piece_firsts(half, order, piece):
        return [half + around_z[dz] * NX for dz in order[piece * GROUPS : (piece + 1) * GROUPS]]

    load_w = pltpu.make_async_copy(w_hbm, w_ref, load_sem.at[0])
    load_h = pltpu.make_async_copy(h_hbm, h_in, load_sem.at[1])
    load_w.start()
    load_h.start()
    loads = {}
    n = 2
    for half in (1, 0):
        for piece in range(PIECES):
            loads[half, piece] = []
            for q in piece_firsts((own_half, other_half)[half], FAR_FIRST, piece):
                copy = pltpu.make_async_copy(c_hbm.at[:, columns(q, NX)], c_ref.at[:, columns(q, NX)], load_sem.at[n])
                copy.start()
                loads[half, piece].append(copy)
                n += 1

    def remote(src, dst, send, recv, to):
        return pltpu.make_async_remote_copy(
            src_ref=src, dst_ref=dst, send_sem=send, recv_sem=recv, device_id=to, device_id_type=MESH
        )

    load_w.wait()
    load_h.wait()
    w = w_ref[...]
    for it in range(ITERS):
        h_next = h_ref.at[it]

        def maps_at(q, count):
            if it == 0:
                return h_in[:, columns(q, count)]
            return jnp.concatenate([h_ref[it - 1, q + i] for i in range(count)], axis=1)

        for_model, for_maps = weight_operands(w)
        row_src[it] = to_row(jnp.sum(w, axis=1, keepdims=True))

        def numerators(half, piece, out):
            firsts = piece_firsts((own_half, other_half)[half], FAR_FIRST, piece)
            if it == 0:
                for copy in loads[half, piece]:
                    copy.wait()
            h = jnp.concatenate([maps_at(q, NX) for q in firsts], axis=1)
            rc, _ = ratios(c_ref, h, for_model, firsts)
            both = jnp.dot(for_maps, rc, preferred_element_type=F32)
            both = both[:K] + both[K:]
            for i in range(PIECE):
                out[piece * PIECE + i] = both[:, i * LANES : (i + 1) * LANES]

        def send_parts(here, part):
            band = pl.ds(part * ROWS, ROWS)
            for slot, (dz, dx) in enumerate(PART_OFFSETS[part]):
                if dz in here:
                    remote(
                        partial.at[it, FAR_FIRST.index(dz) * NX + around_x[dx], band],
                        parts.at[it, part, slot],
                        part_send.at[it, part], part_recv.at[it, part], device(dz, dx),
                    ).start()

        row_copy = remote(row_src.at[it], row_core.at[it], rowc_send.at[it], rowc_recv.at[it], sibling)
        if it:
            row_copy.start()
        core_copies = []
        for piece in range(PIECES):
            numerators(1, piece, numer.at[it])
            if it == 0 and piece == 0:
                pl.semaphore_wait(barrier, len(OFFSETS) + 1 + len(y_devices))
                row_copy.start()
            chunks = pl.ds(piece * PIECE, PIECE)
            copy = remote(
                numer.at[it, chunks], from_core.at[it, chunks],
                core_send.at[it, piece], core_recv.at[it, piece], sibling,
            )
            copy.start()
            core_copies.append(copy)
        for piece in range(PIECES):
            numerators(0, piece, partial.at[it])
            if piece == 0:
                row_copy.wait()
                row_sum[it] = row_src[it] + row_core[it]
                for offset in OFFSETS:
                    remote(
                        row_sum.at[it], rows.at[it, SLOT[offset]], row_send.at[it], row_recv.at[it], device(*offset)
                    ).start()
            core_copies[piece].wait()
            chunks = pl.ds(piece * PIECE, PIECE)
            partial[it, chunks] = partial[it, chunks] + from_core[it, chunks]
            here = FAR_FIRST[piece * GROUPS : (piece + 1) * GROUPS]
            for i, dz in enumerate(VIA_X):
                if dz in here:
                    for j, dx in enumerate(X_OFFSETS):
                        remote(
                            partial.at[it, FAR_FIRST.index(dz) * NX + around_x[dx], last_band], along_x.at[it, i, j],
                            along_x_send.at[it], along_x_recv.at[it, i], device(0, dx),
                        ).start()
            send_parts(here, 0)
        for part in range(1, PARTS):
            send_parts(FAR_FIRST, part)
        for i, dz in enumerate(VIA_X):
            landed = along_x.at[it, i]
            pltpu.make_async_copy(landed, landed, along_x_recv.at[it, i]).wait()
            x_sum[it, i] = partial[it, FAR_FIRST.index(dz) * NX + x, last_band] + jnp.sum(along_x[it, i], axis=0)
            remote(x_sum.at[it, i], along_z.at[it, i], along_z_send.at[it], along_z_recv.at[it], device(dz, 0)).start()

        pltpu.make_async_copy(rows.at[it], rows.at[it], row_recv.at[it]).wait()
        c_total = to_column(row_sum[it] + jnp.sum(rows[it], axis=0))
        scale = maps_at(mine, 1) / c_total
        for part in range(PARTS):
            band = pl.ds(part * ROWS, ROWS)
            count = len(PART_OFFSETS[part])
            landed = parts.at[it, part, pl.ds(0, count)]
            pltpu.make_async_copy(landed, landed, part_recv.at[it, part]).wait()
            numer_total = partial[it, FAR_FIRST.index(0) * NX + x, band] + jnp.sum(parts[it, part, :count], axis=0)
            if VIA_X and part == LAST:
                pltpu.make_async_copy(along_z.at[it], along_z.at[it], along_z_recv.at[it]).wait()
                numer_total += jnp.sum(along_z[it], axis=0)
            h_next[mine, band] = scale[part * ROWS : (part + 1) * ROWS] * numer_total
            chunk = h_next.at[mine, band]
            if part == 0:
                for dz in VIA_Z:
                    remote(chunk, chunk, first_send.at[it], first_recv.at[it, (NZ - dz) % NZ], device(dz, 0)).start()
            for dz, dx in OFFSETS:
                if part or dz not in VIA_Z:
                    remote(chunk, chunk, map_send.at[it], map_recv.at[it, (NZ - dz) % NZ], device(dz, dx)).start()
        for dz in VIA_Z[::-1]:
            chunk = h_next.at[own_half + around_z[dz] * NX + x, pl.ds(0, ROWS)]
            pltpu.make_async_copy(chunk, chunk, first_recv.at[it, dz]).wait()
            for dx in X_OFFSETS:
                remote(chunk, chunk, first_send.at[it], map_recv.at[it, dz], device(0, dx)).start()

        total, sums = jnp.zeros((2 * K, 2 * FRAMES), F32), jnp.zeros((K, LANES), F32)

        def weight_numerators(half, piece, total, sums):
            firsts = piece_firsts((own_half, other_half)[half], NEAR_FIRST, piece)
            h = jnp.concatenate([h_next[q + i] for q in firsts for i in range(NX)], axis=1)
            rc, hc = ratios(c_ref, h, for_model, firsts)
            total += lax.dot_general(hc, rc, (((1,), (1,)), ((), ())), preferred_element_type=F32)
            for i in range(PIECE):
                sums += h[:, i * LANES : (i + 1) * LANES]
            return total, sums

        half_copies = []
        for piece in range(PIECES):
            for dz in NEAR_FIRST[piece * GROUPS : (piece + 1) * GROUPS]:
                group = h_next.at[pl.ds(own_half + around_z[dz] * NX, NX)]
                bands = 6 if dz == 0 else 7 if dz in VIA_Z else 8
                landed = parts.at[it, 0, pl.ds(0, bands)]
                pltpu.make_async_copy(landed, landed, map_recv.at[it, dz]).wait()
                copy = remote(group, group, half_send.at[it, dz], half_recv.at[it, dz], sibling)
                copy.start()
                half_copies.append(copy)
            total, sums = weight_numerators(0, piece, total, sums)
        for piece in range(PIECES):
            for copy in half_copies[piece * GROUPS : (piece + 1) * GROUPS]:
                copy.wait_recv()
            total, sums = weight_numerators(1, piece, total, sums)
        total = total[:K] + total[K:]
        total = total[:, :FRAMES] + total[:, FRAMES:]
        h_total = jnp.sum(sums, axis=1, keepdims=True)
        y_src[it] = jnp.concatenate([total, jnp.broadcast_to(h_total, (K, LANES - FRAMES))], axis=1)
        for i, to in enumerate(y_devices):
            remote(y_src.at[it], y_parts.at[it, i], y_send.at[it], y_recv.at[it], to).start()
        if it == ITERS - 1:
            for i in range(2 * HALF):
                h_in[:, i * LANES : (i + 1) * LANES] = h_next[i]
            store_h = pltpu.make_async_copy(h_in, h_out, load_sem.at[0])
            store_h.start()
        pltpu.make_async_copy(rows.at[it], rows.at[it], row_send.at[it]).wait()
        for part in range(PARTS):
            landed = parts.at[it, part, pl.ds(0, len(PART_OFFSETS[part]))]
            pltpu.make_async_copy(landed, landed, part_send.at[it, part]).wait()
        if VIA_X:
            pltpu.make_async_copy(along_x.at[it], along_x.at[it], along_x_send.at[it]).wait()
            pltpu.make_async_copy(along_z.at[it], along_z.at[it], along_z_send.at[it]).wait()
        landed = h_next.at[pl.ds(0, len(OFFSETS) - 2 * len(VIA_Z))]
        pltpu.make_async_copy(landed, landed, map_send.at[it]).wait()
        if VIA_Z:
            landed = h_next.at[pl.ds(0, 2 * len(VIA_Z))]
            pltpu.make_async_copy(landed, landed, first_send.at[it]).wait()
        for copy in half_copies:
            copy.wait_send()
        pltpu.make_async_copy(y_parts.at[it], y_parts.at[it], y_recv.at[it]).wait()
        total = y_src[it] + jnp.sum(y_parts[it], axis=0)
        w = w * total[:, :FRAMES] / total[:, FRAMES : FRAMES + 1]
        pltpu.make_async_copy(y_parts.at[it], y_parts.at[it], y_send.at[it]).wait()
    w_out[...] = w
    store_h.wait()


def local(counts, weights, maps):
    n = len(OFFSETS)
    dma = pltpu.SemaphoreType.DMA
    anywhere = pl.BlockSpec(memory_space=pl.ANY)
    w_new, h_new = pl.pallas_call(
        kernel,
        out_shape=(jax.ShapeDtypeStruct(weights.shape, F32), jax.ShapeDtypeStruct(maps.shape, F32)),
        in_specs=[anywhere] * 3,
        out_specs=(pl.BlockSpec(memory_space=pltpu.VMEM), anywhere),
        scratch_shapes=[
            pltpu.VMEM((FRAMES, PIX), jnp.int32),
            pltpu.VMEM((K, FRAMES), F32),
            pltpu.VMEM((K, PIX), F32),
            pltpu.VMEM((ITERS, 2 * HALF, K, LANES), F32),
            pltpu.VMEM((ITERS, HALF, K, LANES), F32),
            pltpu.VMEM((ITERS, HALF, K, LANES), F32),
            pltpu.VMEM((ITERS, HALF, K, LANES), F32),
            pltpu.VMEM((ITERS, PARTS, n, ROWS, LANES), F32),
            pltpu.VMEM((ITERS, 1, LANES), F32),
            pltpu.VMEM((ITERS, 1, LANES), F32),
            pltpu.VMEM((ITERS, 1, LANES), F32),
            pltpu.VMEM((ITERS, n, 1, LANES), F32),
            pltpu.VMEM((ITERS, K, LANES), F32),
            pltpu.VMEM((ITERS, NY - 1, K, LANES), F32),
            pltpu.VMEM((ITERS, STAGED, NX - 1, ROWS, LANES), F32),
            pltpu.VMEM((ITERS, STAGED, ROWS, LANES), F32),
            pltpu.VMEM((ITERS, STAGED, ROWS, LANES), F32),
            dma((ITERS,)),
            dma((ITERS, STAGED)),
            dma((ITERS,)),
            dma((ITERS,)),
            dma((ITERS,)),
            dma((ITERS, NZ)),
            dma((2 + 2 * NZ,)),
            dma((ITERS, PIECES)),
            dma((ITERS, PIECES)),
            dma((ITERS, PARTS)),
            dma((ITERS, PARTS)),
            dma((ITERS,)),
            dma((ITERS, NZ)),
            dma((ITERS, NZ)),
            dma((ITERS, NZ)),
            dma((ITERS,)),
            dma((ITERS,)),
            dma((ITERS,)),
            dma((ITERS,)),
            dma((ITERS,)),
            dma((ITERS,)),
        ],
        compiler_params=pltpu.CompilerParams(
            collective_id=0, has_side_effects=True, vmem_limit_bytes=53 * 1024 * 1024
        ),
        name="nmf_updates",
    )(counts, weights, maps)
    return pl.pallas_call(
        store,
        out_shape=(jax.ShapeDtypeStruct(weights.shape, F32), jax.ShapeDtypeStruct(maps.shape, F32)),
        in_specs=[pl.BlockSpec(memory_space=pltpu.VMEM)] * 2,
        out_specs=(anywhere, anywhere),
        scratch_shapes=[dma((2,))],
        compiler_params=pltpu.CompilerParams(vmem_limit_bytes=4 * 1024 * 1024),
        name="store_outputs",
    )(w_new, h_new)


def store(w_in, h_in, w_out, h_out, sems):
    copies = [pltpu.make_async_copy(w_in, w_out, sems.at[0]), pltpu.make_async_copy(h_in, h_out, sems.at[1])]
    for copy in copies:
        copy.start()
    for copy in copies:
        copy.wait()


def solution(mesh):
    return jax.shard_map(
        local,
        mesh=mesh,
        in_specs=(P("frames", "pix"), P(None, "frames"), P(None, "pix")),
        out_specs=(P(None, "frames"), P(None, "pix")),
        check_vma=False,
    )
```

```python
import functools

import jax
import jax.numpy as jnp
from jax import lax
from jax.experimental import pallas as pl
from jax.experimental.pallas import tpu as pltpu
from jax.sharding import PartitionSpec as P

MESH = pl.DeviceIdType.MESH
F32 = jnp.float32
BF16 = jnp.bfloat16
ITERS = 2
NZ, NX, NY = 8, 4, 8
K = 16
LANES = 128
FRAMES = 64
HALF = NZ * NX
PIX = 2 * HALF * LANES


def hops(offset):
    dz, dx = offset
    return min(dz, NZ - dz) + min(dx, NX - dx)


OFFSETS = sorted(((dz, dx) for dz in range(NZ) for dx in range(NX) if dz or dx), key=lambda o: (-min(o[1], NX - o[1]), -min(o[0], NZ - o[0])))
SLOT = {offset: i for i, offset in enumerate(OFFSETS)}
Y_OFFSETS = (4, 3, 5, 2, 6, 1, 7)
FAR_FIRST = (4, 3, 5, 2, 6, 1, 7, 0)
GATHERED = ((0, 1, 7), (2, 6, 3), (5, 4))
ORDER = (('forward', 0), ('own', 0), ('forward', 1), ('forward', 2), ('own', 1), ('sibling', 0), ('own', 2), ('sibling', 1), ('sibling', 2))
GROUPS = 4
PIECES = NZ // GROUPS
GROUP_PIX = NX * LANES
PIECE = GROUPS * NX
PARTS = 2
VIA_X = (4, 3, 5, 2, 6, 1, 7)
VIA_Z = (4, 3, 5, 2, 6, 1, 7)
ROWS = K // PARTS
LAST = PARTS - 1
STAGED = max(1, len(VIA_X))
X_OFFSETS = (2, 1, 3)
PART_OFFSETS = [[o for o in sorted(OFFSETS, key=lambda o: -hops(o)) if part < LAST or o[0] not in VIA_X] for part in range(PARTS)]


def split(x):
    hi = x.astype(BF16)
    return hi, (x - hi.astype(F32)).astype(BF16)


def weight_operands(w):
    hi, lo = split(w)
    for_model = jnp.concatenate([hi, hi, lo, lo], axis=0)
    for_maps = jnp.concatenate([jnp.concatenate([hi, hi], axis=1), jnp.concatenate([lo, lo], axis=1)], axis=0)
    return for_model, for_maps


def columns(chunk, count):
    return pl.ds(pl.multiple_of(chunk * LANES, count * LANES), count * LANES)


def ratios(c_ref, h, for_model, firsts):
    hi, lo = split(h)
    model = lax.dot_general(
        for_model,
        jnp.concatenate([hi, lo, hi, lo], axis=0),
        (((0,), (0,)), ((), ())),
        preferred_element_type=F32,
    )
    counts = jnp.concatenate([c_ref[:, columns(q, NX)] for q in firsts], axis=1).astype(F32)
    r_hi, r_lo = split(counts / model)
    return jnp.concatenate([r_hi, r_lo], axis=0), jnp.concatenate([hi, lo], axis=0)


def to_row(column):
    shape = (K, LANES)
    diagonal = lax.broadcasted_iota(jnp.int32, shape, 0) == lax.broadcasted_iota(jnp.int32, shape, 1)
    return jnp.sum(jnp.where(diagonal, column, 0.0), axis=0, keepdims=True)


def to_column(row):
    shape = (K, LANES)
    diagonal = lax.broadcasted_iota(jnp.int32, shape, 0) == lax.broadcasted_iota(jnp.int32, shape, 1)
    return jnp.sum(jnp.where(diagonal, row, 0.0), axis=1, keepdims=True)


def kernel(
    c_hbm, w_hbm, h_hbm, w_out, h_out,
    c_ref, w_ref, h_in, h_ref, numer, from_core, partial, parts, row_src, row_core, row_sum, rows, y_src, y_parts,
    along_x, x_sum, along_z, along_x_send, along_x_recv, along_z_send, along_z_recv, first_send, first_recv,
    load_sem, core_send, core_recv, part_send, part_recv, map_send, map_recv, half_send, half_recv,
    rowc_send, rowc_recv, row_send, row_recv, y_send, y_recv,
):
    f = lax.axis_index("frames")
    y = lax.axis_index("pix")
    z, x, core = f // (2 * NX), lax.rem(f // 2, NX), lax.rem(f, 2)
    around_z = [lax.rem(z + d, NZ) for d in range(NZ)]
    around_x = [lax.rem(x + d, NX) for d in range(NX)]

    def device(dz, dx):
        return ((around_z[dz] * NX + around_x[dx]) * 2 + core, y)

    sibling = (f + 1 - 2 * core, y)
    y_devices = [(f, lax.rem(y + d, NY)) for d in Y_OFFSETS]
    own_half = core * HALF
    last_band = pl.ds(LAST * ROWS, ROWS)
    other_half = (1 - core) * HALF
    mine = own_half + z * NX + x

    barrier = pltpu.get_barrier_semaphore()
    for offset in OFFSETS:
        pl.semaphore_signal(barrier, inc=1, device_id=device(*offset), device_id_type=MESH)
    for d in [sibling] + y_devices:
        pl.semaphore_signal(barrier, inc=1, device_id=d, device_id_type=MESH)

    def piece_firsts(half, order, piece):
        return [half + around_z[dz] * NX for dz in order[piece * GROUPS : (piece + 1) * GROUPS]]

    load_w = pltpu.make_async_copy(w_hbm, w_ref, load_sem.at[0])
    load_h = pltpu.make_async_copy(h_hbm, h_in, load_sem.at[1])
    load_w.start()
    load_h.start()
    loads = {}
    n = 2
    for half in (1, 0):
        for piece in range(PIECES):
            loads[half, piece] = []
            for q in piece_firsts((own_half, other_half)[half], FAR_FIRST, piece):
                copy = pltpu.make_async_copy(c_hbm.at[:, columns(q, NX)], c_ref.at[:, columns(q, NX)], load_sem.at[n])
                copy.start()
                loads[half, piece].append(copy)
                n += 1

    def remote(src, dst, send, recv, to):
        return pltpu.make_async_remote_copy(
            src_ref=src, dst_ref=dst, send_sem=send, recv_sem=recv, device_id=to, device_id_type=MESH
        )

    load_w.wait()
    load_h.wait()
    w = w_ref[...]
    for it in range(ITERS):
        h_next = h_ref.at[it]

        def maps_at(q, count):
            if it == 0:
                return h_in[:, columns(q, count)]
            return jnp.concatenate([h_ref[it - 1, q + i] for i in range(count)], axis=1)

        for_model, for_maps = weight_operands(w)
        row_src[it] = to_row(jnp.sum(w, axis=1, keepdims=True))

        def numerators(half, piece, out):
            firsts = piece_firsts((own_half, other_half)[half], FAR_FIRST, piece)
            if it == 0:
                for copy in loads[half, piece]:
                    copy.wait()
            h = jnp.concatenate([maps_at(q, NX) for q in firsts], axis=1)
            rc, _ = ratios(c_ref, h, for_model, firsts)
            both = jnp.dot(for_maps, rc, preferred_element_type=F32)
            both = both[:K] + both[K:]
            for i in range(PIECE):
                out[piece * PIECE + i] = both[:, i * LANES : (i + 1) * LANES]

        def send_parts(here, part):
            band = pl.ds(part * ROWS, ROWS)
            for slot, (dz, dx) in enumerate(PART_OFFSETS[part]):
                if dz in here:
                    remote(
                        partial.at[it, FAR_FIRST.index(dz) * NX + around_x[dx], band],
                        parts.at[it, part, slot],
                        part_send.at[it, part], part_recv.at[it, part], device(dz, dx),
                    ).start()

        row_copy = remote(row_src.at[it], row_core.at[it], rowc_send.at[it], rowc_recv.at[it], sibling)
        if it:
            row_copy.start()
        core_copies = []
        for piece in range(PIECES):
            numerators(1, piece, numer.at[it])
            if it == 0 and piece == 0:
                pl.semaphore_wait(barrier, len(OFFSETS) + 1 + len(y_devices))
                row_copy.start()
            chunks = pl.ds(piece * PIECE, PIECE)
            copy = remote(
                numer.at[it, chunks], from_core.at[it, chunks],
                core_send.at[it, piece], core_recv.at[it, piece], sibling,
            )
            copy.start()
            core_copies.append(copy)
        for piece in range(PIECES):
            numerators(0, piece, partial.at[it])
            if piece == 0:
                row_copy.wait()
                row_sum[it] = row_src[it] + row_core[it]
                for offset in OFFSETS:
                    remote(
                        row_sum.at[it], rows.at[it, SLOT[offset]], row_send.at[it], row_recv.at[it], device(*offset)
                    ).start()
            core_copies[piece].wait()
            chunks = pl.ds(piece * PIECE, PIECE)
            partial[it, chunks] = partial[it, chunks] + from_core[it, chunks]
            here = FAR_FIRST[piece * GROUPS : (piece + 1) * GROUPS]
            for i, dz in enumerate(VIA_X):
                if dz in here:
                    for j, dx in enumerate(X_OFFSETS):
                        remote(
                            partial.at[it, FAR_FIRST.index(dz) * NX + around_x[dx], last_band], along_x.at[it, i, j],
                            along_x_send.at[it], along_x_recv.at[it, i], device(0, dx),
                        ).start()
            send_parts(here, 0)
        for part in range(1, PARTS):
            send_parts(FAR_FIRST, part)
        for i, dz in enumerate(VIA_X):
            landed = along_x.at[it, i]
            pltpu.make_async_copy(landed, landed, along_x_recv.at[it, i]).wait()
            x_sum[it, i] = partial[it, FAR_FIRST.index(dz) * NX + x, last_band] + jnp.sum(along_x[it, i], axis=0)
            remote(x_sum.at[it, i], along_z.at[it, i], along_z_send.at[it], along_z_recv.at[it], device(dz, 0)).start()

        pltpu.make_async_copy(rows.at[it], rows.at[it], row_recv.at[it]).wait()
        c_total = to_column(row_sum[it] + jnp.sum(rows[it], axis=0))
        scale = maps_at(mine, 1) / c_total
        for part in range(PARTS):
            band = pl.ds(part * ROWS, ROWS)
            count = len(PART_OFFSETS[part])
            landed = parts.at[it, part, pl.ds(0, count)]
            pltpu.make_async_copy(landed, landed, part_recv.at[it, part]).wait()
            numer_total = partial[it, FAR_FIRST.index(0) * NX + x, band] + jnp.sum(parts[it, part, :count], axis=0)
            if VIA_X and part == LAST:
                pltpu.make_async_copy(along_z.at[it], along_z.at[it], along_z_recv.at[it]).wait()
                numer_total += jnp.sum(along_z[it], axis=0)
            h_next[mine, band] = scale[part * ROWS : (part + 1) * ROWS] * numer_total
            chunk = h_next.at[mine, band]
            if part == 0:
                for dz in VIA_Z:
                    remote(chunk, chunk, first_send.at[it], first_recv.at[it, (NZ - dz) % NZ], device(dz, 0)).start()
            for dz, dx in OFFSETS:
                if part or dz not in VIA_Z:
                    remote(chunk, chunk, map_send.at[it], map_recv.at[it, (NZ - dz) % NZ], device(dz, dx)).start()
        for dz in VIA_Z[::-1]:
            chunk = h_next.at[own_half + around_z[dz] * NX + x, pl.ds(0, ROWS)]
            pltpu.make_async_copy(chunk, chunk, first_recv.at[it, dz]).wait()
            for dx in X_OFFSETS:
                remote(chunk, chunk, first_send.at[it], map_recv.at[it, dz], device(0, dx)).start()

        total, sums = jnp.zeros((2 * K, 2 * FRAMES), F32), jnp.zeros((K, LANES), F32)

        def weight_numerators(half, groups, total, sums):
            firsts = [(own_half, other_half)[half] + around_z[dz] * NX for dz in groups]
            h = jnp.concatenate([h_next[q + i] for q in firsts for i in range(NX)], axis=1)
            rc, hc = ratios(c_ref, h, for_model, firsts)
            total += lax.dot_general(hc, rc, (((1,), (1,)), ((), ())), preferred_element_type=F32)
            for i in range(len(groups) * NX):
                sums += h[:, i * LANES : (i + 1) * LANES]
            return total, sums

        half_copies = {}
        for step, piece in ORDER:
            groups = GATHERED[piece]
            if step == "forward":
                for dz in groups:
                    group = h_next.at[pl.ds(own_half + around_z[dz] * NX, NX)]
                    bands = 6 if dz == 0 else 7 if dz in VIA_Z else 8
                    landed = parts.at[it, 0, pl.ds(0, bands)]
                    pltpu.make_async_copy(landed, landed, map_recv.at[it, dz]).wait()
                    half_copies[dz] = remote(group, group, half_send.at[it, dz], half_recv.at[it, dz], sibling)
                    half_copies[dz].start()
            elif step == "own":
                total, sums = weight_numerators(0, groups, total, sums)
            else:
                for dz in groups:
                    half_copies[dz].wait_recv()
                total, sums = weight_numerators(1, groups, total, sums)
        total = total[:K] + total[K:]
        total = total[:, :FRAMES] + total[:, FRAMES:]
        h_total = jnp.sum(sums, axis=1, keepdims=True)
        y_src[it] = jnp.concatenate([total, jnp.broadcast_to(h_total, (K, LANES - FRAMES))], axis=1)
        for i, to in enumerate(y_devices):
            remote(y_src.at[it], y_parts.at[it, i], y_send.at[it], y_recv.at[it], to).start()
        if it == ITERS - 1:
            for i in range(2 * HALF):
                h_in[:, i * LANES : (i + 1) * LANES] = h_next[i]
            store_h = pltpu.make_async_copy(h_in, h_out, load_sem.at[0])
            store_h.start()
        pltpu.make_async_copy(rows.at[it], rows.at[it], row_send.at[it]).wait()
        for part in range(PARTS):
            landed = parts.at[it, part, pl.ds(0, len(PART_OFFSETS[part]))]
            pltpu.make_async_copy(landed, landed, part_send.at[it, part]).wait()
        if VIA_X:
            pltpu.make_async_copy(along_x.at[it], along_x.at[it], along_x_send.at[it]).wait()
            pltpu.make_async_copy(along_z.at[it], along_z.at[it], along_z_send.at[it]).wait()
        landed = h_next.at[pl.ds(0, len(OFFSETS) - 2 * len(VIA_Z))]
        pltpu.make_async_copy(landed, landed, map_send.at[it]).wait()
        if VIA_Z:
            landed = h_next.at[pl.ds(0, 2 * len(VIA_Z))]
            pltpu.make_async_copy(landed, landed, first_send.at[it]).wait()
        for copy in half_copies.values():
            copy.wait_send()
        pltpu.make_async_copy(y_parts.at[it], y_parts.at[it], y_recv.at[it]).wait()
        total = y_src[it] + jnp.sum(y_parts[it], axis=0)
        w = w * total[:, :FRAMES] / total[:, FRAMES : FRAMES + 1]
        pltpu.make_async_copy(y_parts.at[it], y_parts.at[it], y_send.at[it]).wait()
    w_out[...] = w
    store_h.wait()


def local(counts, weights, maps):
    n = len(OFFSETS)
    dma = pltpu.SemaphoreType.DMA
    anywhere = pl.BlockSpec(memory_space=pl.ANY)
    w_new, h_new = pl.pallas_call(
        kernel,
        out_shape=(jax.ShapeDtypeStruct(weights.shape, F32), jax.ShapeDtypeStruct(maps.shape, F32)),
        in_specs=[anywhere] * 3,
        out_specs=(pl.BlockSpec(memory_space=pltpu.VMEM), anywhere),
        scratch_shapes=[
            pltpu.VMEM((FRAMES, PIX), jnp.int32),
            pltpu.VMEM((K, FRAMES), F32),
            pltpu.VMEM((K, PIX), F32),
            pltpu.VMEM((ITERS, 2 * HALF, K, LANES), F32),
            pltpu.VMEM((ITERS, HALF, K, LANES), F32),
            pltpu.VMEM((ITERS, HALF, K, LANES), F32),
            pltpu.VMEM((ITERS, HALF, K, LANES), F32),
            pltpu.VMEM((ITERS, PARTS, n, ROWS, LANES), F32),
            pltpu.VMEM((ITERS, 1, LANES), F32),
            pltpu.VMEM((ITERS, 1, LANES), F32),
            pltpu.VMEM((ITERS, 1, LANES), F32),
            pltpu.VMEM((ITERS, n, 1, LANES), F32),
            pltpu.VMEM((ITERS, K, LANES), F32),
            pltpu.VMEM((ITERS, NY - 1, K, LANES), F32),
            pltpu.VMEM((ITERS, STAGED, NX - 1, ROWS, LANES), F32),
            pltpu.VMEM((ITERS, STAGED, ROWS, LANES), F32),
            pltpu.VMEM((ITERS, STAGED, ROWS, LANES), F32),
            dma((ITERS,)),
            dma((ITERS, STAGED)),
            dma((ITERS,)),
            dma((ITERS,)),
            dma((ITERS,)),
            dma((ITERS, NZ)),
            dma((2 + 2 * NZ,)),
            dma((ITERS, PIECES)),
            dma((ITERS, PIECES)),
            dma((ITERS, PARTS)),
            dma((ITERS, PARTS)),
            dma((ITERS,)),
            dma((ITERS, NZ)),
            dma((ITERS, NZ)),
            dma((ITERS, NZ)),
            dma((ITERS,)),
            dma((ITERS,)),
            dma((ITERS,)),
            dma((ITERS,)),
            dma((ITERS,)),
            dma((ITERS,)),
        ],
        compiler_params=pltpu.CompilerParams(
            collective_id=0, has_side_effects=True, vmem_limit_bytes=53 * 1024 * 1024
        ),
        name="nmf_updates",
    )(counts, weights, maps)
    return pl.pallas_call(
        store,
        out_shape=(jax.ShapeDtypeStruct(weights.shape, F32), jax.ShapeDtypeStruct(maps.shape, F32)),
        in_specs=[pl.BlockSpec(memory_space=pltpu.VMEM)] * 2,
        out_specs=(anywhere, anywhere),
        scratch_shapes=[dma((2,))],
        compiler_params=pltpu.CompilerParams(vmem_limit_bytes=4 * 1024 * 1024),
        name="store_outputs",
    )(w_new, h_new)


def store(w_in, h_in, w_out, h_out, sems):
    copies = [pltpu.make_async_copy(w_in, w_out, sems.at[0]), pltpu.make_async_copy(h_in, h_out, sems.at[1])]
    for copy in copies:
        copy.start()
    for copy in copies:
        copy.wait()


def solution(mesh):
    return jax.shard_map(
        local,
        mesh=mesh,
        in_specs=(P("frames", "pix"), P(None, "frames"), P(None, "pix")),
        out_specs=(P(None, "frames"), P(None, "pix")),
        check_vma=False,
    )
```
